32 devices in a mesh: groups: 2 (over y), ctx: 4 (over z), tp: 4 (over x, core).
Axes of the slice: x: 2, y: 2, z: 4, core: 2. Of those that a mesh axis runs over, the one named last changes fastest.
Arguments:
- tokens: bfloat16 [2048, 4096], P(('groups', 'ctx', 'tp')), parts along dimension 0, may hold values from -6 to 6
- gain: float32 [4096], replicated, may hold values from 0.4 to 1.6
- wq: bfloat16 [4096, 4096], P('ctx', 'tp'), may hold values from -0.046875 to 0.046875
- wk: bfloat16 [4096, 1024], P('ctx', 'tp'), may hold values from -1.421875 to 1.421875
- wv: bfloat16 [4096, 1024], P('ctx', 'tp'), may hold values from -0.09375 to 0.09375
- wo: bfloat16 [4096, 4096], P('tp'), may hold values from -0.09375 to 0.09375
- sections: int32 [2048], P('groups'), parts along dimension 0, may hold values from 0 to 6, as said below
Outputs:
- attention_out: bfloat16 [2048, 4096], P(('groups', 'ctx', 'tp')), parts along dimension 0
The draws below stay inside these ranges and needn't reach their ends.
There are 2 independent parts, one for each index of `groups`. The reference program is written for one: setup_inputs(seed, part) draws one part's arguments, and reference() takes and returns one part's arrays. A program takes and returns all parts, laid end to end along the dimension named above; an argument that names none is the same for every part. Nothing has to cross between parts.
Inputs may be any that keep to these rules, and one draw needn't show every extreme that they name: sections starts at 0, never falls, rises by at most 1 from one token to the next, and the last token has section 6.
All inputs are finite; a program needn't handle non-finite values.
Results may differ from the reference program's by a relative error of at most 0.01.
The reference program's roundings to bfloat16 on the way count: a program that leaves them out, or rounds other values in their place, can miss the bound.
Values may be sent and summed in bfloat16 or wider, within the bound.
A program may use at most 128 MiB of HBM per device.

```python
import math
import jax
import jax.numpy as jnp
from jax import lax

D = 4096
HEADS = 32
KV = 8
HD = 128
TOTAL = 1024
N_TP = 4


def shared_query(key):
    return jnp.clip(jax.random.normal(key, (D, HEADS * HD), jnp.float32), -3.0, 3.0)


def draw_wq(key, part):
    base = shared_query(key)
    return (base * D ** (-0.5)).astype(jnp.bfloat16)


def draw_wk(key, part):
    key = jax.random.fold_in(key, 12)
    own_key = jax.random.fold_in(key, 0)
    own = jnp.clip(jax.random.normal(own_key, (D, KV * HD), jnp.float32), -3.0, 3.0) * D ** (-0.5)
    return own.astype(jnp.bfloat16)


def draw_sections(key, part):
    key = jax.random.fold_in(key, 13)
    places = jax.random.permutation(key, TOTAL - 1)[:6] + 1
    flags = jnp.zeros((TOTAL,), jnp.int32).at[places].set(1)
    return jnp.cumsum(flags).astype(jnp.int32)


def steps_of(stream_key, shape, shards, low, largest):
    factor_of = 1.0
    for axis_at, parts in shards:
        steps = jax.random.uniform(jax.random.fold_in(jax.random.fold_in(stream_key, 6), axis_at), (parts,), jnp.float32, low / len(shards), largest / len(shards))
        factor_of = factor_of * jnp.repeat(jnp.exp(steps), shape[axis_at] // parts).reshape((-1,) + (1,) * (len(shape) - 1 - axis_at))
    return factor_of


def gaussian(key, dims, deviation, limit, cuts=(), held_as=jnp.bfloat16):
    level = steps_of(key, dims, cuts, -0.22, 0.18) if cuts else 1.0
    values = jax.random.normal(key, dims, jnp.float32) * deviation * level
    return jnp.minimum(jnp.maximum(values, -limit), limit).astype(held_as)


def setup_inputs(seed: int = 0, part: int = 0) -> dict:
    streams_of = jax.random.split(jax.random.key(seed), 8)
    own_keys = jax.random.split(jax.random.fold_in(streams_of[7], part), 8)
    return {
        "tokens": gaussian(own_keys[0], (TOTAL, D), 1.0, 6.0, ((0, 16),)),
        "gain": jnp.clip(1.0 + 0.12 * jax.random.normal(streams_of[1], (D,), jnp.float32), 0.4, 1.6),
        "wq": draw_wq(jax.random.fold_in(streams_of[7], 71), part),
        "wk": draw_wk(jax.random.fold_in(streams_of[7], 71), part),
        "wv": gaussian(streams_of[4], (D, KV * HD), D ** -0.5, 0.09375, ((0, 4), (1, 4))),
        "wo": gaussian(streams_of[5], (HEADS * HD, D), (HEADS * HD) ** -0.5, 0.09375, ((0, 4),)),
        "sections": draw_sections(jax.random.fold_in(jax.random.fold_in(streams_of[7], part), 71), part),
    }


theta_base = 500000.0
eps_norm = 1e-05
neg_big = -1e+30

def rotate(values, positions):
    half_dim = values.shape[-1] // 2
    freq = theta_base ** (-(jnp.arange(half_dim, dtype=jnp.float32) * 2.0 / values.shape[-1]))
    angle = positions.astype(jnp.float32)[:, None] * freq[None, :]
    cosine = jnp.cos(angle)[:, None, :]
    sine = jnp.sin(angle)[:, None, :]
    first = values[..., :half_dim]
    second = values[..., half_dim:]
    return jnp.concatenate([first * cosine - second * sine, second * cosine + first * sine], axis=-1)

def norm_rows(tokens, gain):
    values = tokens.astype(jnp.float32)
    meansq = lax.optimization_barrier(jnp.mean(values * values, axis=-1, keepdims=True))
    return (values * lax.rsqrt(meansq + eps_norm) * gain.astype(jnp.float32)).astype(jnp.bfloat16)

def allowed(query_pos, query_section, key_pos, key_section):
    causal = key_pos[None, :] <= query_pos[:, None]
    same_example = key_section[None, :] // 3 == query_section[:, None] // 3
    visible = (key_section[None, :] % 3 == 0) | (key_section[None, :] == query_section[:, None])
    return causal & same_example & visible

def reference(tokens, gain, wq, wk, wv, wo, sections):
    total_len = tokens.shape[0]
    normalized = norm_rows(tokens, gain)
    positions = jnp.arange(total_len, dtype=jnp.int32)
    queries = rotate(jnp.dot(normalized, wq, preferred_element_type=jnp.float32).reshape(total_len, HEADS, HD), positions).astype(jnp.bfloat16)
    keys = rotate(jnp.dot(normalized, wk, preferred_element_type=jnp.float32).reshape(total_len, KV, HD), positions).astype(jnp.bfloat16)
    values = jnp.dot(normalized, wv, preferred_element_type=jnp.float32).astype(jnp.bfloat16).reshape(total_len, KV, HD)
    group_size = HEADS // KV
    block_rows = min(total_len, 1024)
    block_count = total_len // block_rows
    query_heads = queries.reshape(block_count, block_rows, KV, group_size, HD).transpose(2, 0, 1, 3, 4)
    key_heads = keys.transpose(1, 0, 2)
    value_heads = values.transpose(1, 0, 2)
    inv_root = 1.0 / math.sqrt(HD)

    def one_head(inputs):
        query_blocks, key_head, value_head = inputs

        def one_block(block_inputs):
            query_block, block_index = block_inputs
            query_pos = block_index * block_rows + jnp.arange(block_rows, dtype=jnp.int32)
            query_section = jnp.take(sections, query_pos)
            mask = allowed(query_pos, query_section, positions, sections)
            scores = jnp.einsum('qgd,kd->qgk', query_block.astype(jnp.float32), key_head.astype(jnp.float32)) * inv_root
            scores = jnp.where(mask[:, None, :], scores, neg_big)
            row_max = lax.optimization_barrier(jnp.max(scores, axis=-1, keepdims=True))
            weights = jnp.where(mask[:, None, :], jnp.exp(scores - row_max), 0.0)
            weight_sum = lax.optimization_barrier(jnp.sum(weights, axis=-1))
            rounded = weights.astype(jnp.bfloat16)
            mixed = jnp.einsum('qgk,kd->qgd', rounded.astype(jnp.float32), value_head.astype(jnp.float32))
            return (mixed / weight_sum[..., None]).astype(jnp.bfloat16)
        return lax.map(one_block, (query_blocks, jnp.arange(block_count, dtype=jnp.int32)))
    attended = lax.map(one_head, (query_heads, key_heads, value_heads))
    attended = attended.transpose(1, 2, 0, 3, 4).reshape(total_len, HEADS * HD)
    width_part = HEADS * HD // N_TP
    summed = jnp.zeros((total_len, D), jnp.float32)
    for part_index in range(N_TP):
        lower = part_index * width_part
        term = jnp.dot(attended[:, lower:lower + width_part], wo[lower:lower + width_part], preferred_element_type=jnp.float32)
        summed = summed + term.astype(jnp.bfloat16).astype(jnp.float32)
    return summed.astype(jnp.bfloat16)
```

```python
import functools
import math

import jax
import jax.numpy as jnp
from jax import lax
from jax.experimental import pallas as pl
from jax.experimental.pallas import tpu as pltpu
from jax.sharding import PartitionSpec as P

HD = 128
MESH = pl.DeviceIdType.MESH
BF = jnp.bfloat16
F32 = jnp.float32

theta_base = 500000.0
eps_norm = 1e-05
neg_big = -1e30


def kernel(
    G, C, T, parts, chunks,
    tok, gain, cos, sin, secq, seck, wq, wk, wv, wo,
    out,
    nf, Wq, Wk, Wv, Wo, Kf, Vf, qbuf, att, term, pair, sib, xin,
    lsem, zsend, zrecv, ysend, yrecv, nsend, nrecv, ksend, krecv,
    s1send, s1recv, s2send, s2recv,
):
    g = lax.axis_index("groups")
    c = lax.axis_index("ctx")
    t = lax.axis_index("tp")
    X = T // 2
    x = t // 2
    core = lax.rem(t, 2)
    R, D = tok.shape
    B = R * T
    Kc, Nq = wq.shape
    Nk = wk.shape[1]
    kv = Nk // HD
    grp = Nq // Nk
    Kh = Kc // G
    part = Nq // parts
    total = seck.shape[1]
    inv_root = 1.0 / math.sqrt(HD)
    has_right = c < C - 1
    has_left = c > 0

    own = pl.ds(pl.multiple_of(c * Kc, Kc), Kc)
    loads = [
        pltpu.make_async_copy(wk, Wk.at[own], lsem.at[0]),
        pltpu.make_async_copy(wv, Wv.at[own], lsem.at[1]),
        pltpu.make_async_copy(wq, Wq.at[own], lsem.at[2]),
        pltpu.make_async_copy(wo, Wo, lsem.at[3]),
    ]
    for load in loads:
        load.start()

    barrier = pltpu.get_barrier_semaphore()

    @pl.when(has_right)
    def _():
        pl.semaphore_signal(barrier, inc=1, device_id={"ctx": c + 1}, device_id_type=MESH)

    @pl.when(has_left)
    def _():
        pl.semaphore_signal(barrier, inc=1, device_id={"ctx": c - 1}, device_id_type=MESH)

    for i in range(1, G):
        pl.semaphore_signal(
            barrier, inc=1, device_id={"groups": lax.rem(g + i, G)}, device_id_type=MESH
        )
    for i in range(1, T):
        pl.semaphore_signal(
            barrier, inc=1, device_id={"tp": lax.rem(t + i, T)}, device_id_type=MESH
        )
    pl.semaphore_wait(
        barrier, G - 1 + T - 1 + has_right.astype(jnp.int32) + has_left.astype(jnp.int32)
    )

    def piece(a, block, half):
        rows = pl.ds(pl.multiple_of(block * Kc + half * Kh, Kh), Kh)
        if a == 0:
            return Wk.at[rows]
        if a == 1:
            return Wv.at[rows]
        return Wq.at[rows, pl.ds((a - 2) * part, part)]

    def z_copy(a, block, right):
        ref = piece(a, block, g)
        return pltpu.make_async_remote_copy(
            src_ref=ref, dst_ref=ref,
            send_sem=zsend.at[a, block, right], recv_sem=zrecv.at[a, block],
            device_id={"ctx": c + 1 if right else c - 1}, device_id_type=MESH,
        )

    def y_copy(a, block, i, half):
        ref = piece(a, block, half)
        return pltpu.make_async_remote_copy(
            src_ref=ref, dst_ref=ref,
            send_sem=ysend.at[a, block, i], recv_sem=yrecv.at[a, block, i],
            device_id={"groups": lax.rem(g + i, G)}, device_id_type=MESH,
        )

    def send_own(a):
        @pl.when(has_right)
        def _():
            z_copy(a, c, 1).start()

        @pl.when(has_left)
        def _():
            z_copy(a, c, 0).start()

    def arrive(pieces, first, last):
        def body(s, carry):
            left = c - 1 - s
            right = c + 1 + s
            for a in pieces:
                @pl.when(left >= 0)
                def _():
                    z_copy(a, left, 1).wait_recv()

                    @pl.when(has_right)
                    def _():
                        z_copy(a, left, 1).start()

                    for i in range(1, G):
                        y_copy(a, left, i, g).start()

                @pl.when(right < C)
                def _():
                    z_copy(a, right, 0).wait_recv()

                    @pl.when(has_left)
                    def _():
                        z_copy(a, right, 0).start()

                    for i in range(1, G):
                        y_copy(a, right, i, g).start()
            return carry

        lax.fori_loop(first, last, body, 0)

    def y_wait(pieces):
        def body(block, carry):
            @pl.when(block != c)
            def _():
                for a in pieces:
                    for i in range(1, G):
                        y_copy(a, block, i, lax.rem(g + G - i, G)).wait_recv()
            return carry

        lax.fori_loop(0, C, body, 0)

    loads[0].wait()
    loads[1].wait()
    send_own(0)
    send_own(1)
    loads[2].wait()
    send_own(2)

    def n_copy(i, who):
        ref = nf.at[pl.ds(pl.multiple_of(who * R, R), R)]
        return pltpu.make_async_remote_copy(
            src_ref=ref, dst_ref=ref, send_sem=nsend.at[i], recv_sem=nrecv.at[i],
            device_id={"tp": lax.rem(t + i, T)}, device_id_type=MESH,
        )

    values = tok[...].astype(F32)
    meansq = jnp.mean(values * values, axis=-1, keepdims=True)
    nf[pl.ds(pl.multiple_of(t * R, R), R), :] = (
        values * lax.rsqrt(meansq + eps_norm) * gain[...]
    ).astype(BF)
    for i in range(1, T):
        n_copy(i, t).start()

    arrive((0, 1), 0, C - 1)
    for j in range(1, parts):
        send_own(2 + j)
    for i in range(1, T):
        n_copy(i, lax.rem(t + T - i, T)).wait_recv()

    def rotated(head):
        a = head[:, : HD // 2]
        b = head[:, HD // 2 :]
        cs = cos[...]
        sn = sin[...]
        return jnp.concatenate([a * cs - b * sn, b * cs + a * sn], axis=-1).astype(BF)

    def kv_rows(block):
        return pl.ds(pl.multiple_of(block * B, B), B)

    def kv_copy(which, block):
        ref = (Kf, Vf)[which].at[kv_rows(block)]
        return pltpu.make_async_remote_copy(
            src_ref=ref, dst_ref=ref,
            send_sem=ksend.at[which, block], recv_sem=krecv.at[which, block],
            device_id={"ctx": c + 1}, device_id_type=MESH,
        )

    y_wait((0, 1))
    raw = jnp.dot(nf[...], Wk[...], preferred_element_type=F32)
    for j in range(kv):
        Kf[kv_rows(c), j * HD : (j + 1) * HD] = rotated(raw[:, j * HD : (j + 1) * HD])
    Vf[kv_rows(c), :] = jnp.dot(nf[...], Wv[...], preferred_element_type=F32).astype(BF)

    @pl.when(has_right)
    def _():
        kv_copy(0, c).start()
        kv_copy(1, c).start()

    def blank(block, carry):
        Kf[kv_rows(block), :] = jnp.zeros((B, Nk), BF)
        Vf[kv_rows(block), :] = jnp.zeros((B, Nk), BF)
        return carry

    lax.fori_loop(c + 1, C, blank, 0)

    arrive((2,), 0, C - 1)

    def kv_arrive(s, carry):
        left = c - 1 - s

        @pl.when(left >= 0)
        def _():
            for which in range(2):
                kv_copy(which, left).wait_recv()

                @pl.when(has_right)
                def _():
                    kv_copy(which, left).start()
        return carry

    lax.fori_loop(0, C - 1, kv_arrive, 0)

    rows_now = max(16, min(B, (256 * 1024) // total))

    def attend(j):
        y_wait((2 + j,))
        raw = jnp.dot(
            nf[...], Wq[:, j * part : (j + 1) * part], preferred_element_type=F32
        )
        for h in range(part // HD):
            qbuf[h, :, :] = rotated(raw[:, h * HD : (h + 1) * HD])
        for h in range(part // HD):
            head = j * (part // HD) + h
            cols = slice((head // grp) * HD, (head // grp + 1) * HD)

            def tile(n, carry):
                rows = pl.ds(pl.multiple_of(n * rows_now, rows_now), rows_now)
                scores = (
                    lax.dot_general(
                        qbuf[h, rows, :], Kf[:, cols], (((1,), (1,)), ((), ())),
                        preferred_element_type=F32,
                    )
                    * inv_root
                )
                pos = c * B + n * rows_now + lax.broadcasted_iota(jnp.int32, (rows_now, total), 0)
                kpos = lax.broadcasted_iota(jnp.int32, (rows_now, total), 1)
                sq = secq[rows, :]
                sk = seck[...]
                third_q = (sq >= 3).astype(jnp.int32) + (sq >= 6).astype(jnp.int32)
                third_k = (sk >= 3).astype(jnp.int32) + (sk >= 6).astype(jnp.int32)
                prompt = sk == third_k * 3
                mask = (kpos <= pos) & (third_k == third_q) & (prompt | (sk == sq))
                scores = jnp.where(mask, scores, neg_big)
                top = jnp.max(scores, axis=-1, keepdims=True)
                weights = jnp.exp(scores - top)
                denom = jnp.sum(weights, axis=-1, keepdims=True)
                mixed = jnp.dot(weights.astype(BF), Vf[:, cols], preferred_element_type=F32)
                att[rows, head * HD : (head + 1) * HD] = (mixed / denom).astype(BF)
                return carry

            if rows_now == B:
                tile(0, 0)
            else:
                lax.fori_loop(0, B // rows_now, tile, 0)

    for j in range(parts):
        if j + 1 < parts:
            arrive((3 + j,), 0, 1)
        attend(j)
        if j + 1 < parts:
            arrive((3 + j,), 1, C - 1)

    loads[3].wait()
    width = D // chunks

    def t_rows(who):
        return pl.ds(pl.multiple_of(who * R, R), R)

    def cols_of(n):
        return pl.ds(n * width, width)

    def s1_copy(n, xi):
        return pltpu.make_async_remote_copy(
            src_ref=term.at[t_rows(xi * 2 + 1 - core), cols_of(n)],
            dst_ref=sib.at[xi, :, cols_of(n)],
            send_sem=s1send.at[n, xi], recv_sem=s1recv.at[n, xi],
            device_id={"tp": x * 2 + 1 - core}, device_id_type=MESH,
        )

    def s2_copy(n, i, source):
        return pltpu.make_async_remote_copy(
            src_ref=pair.at[i - 1, :, cols_of(n)],
            dst_ref=xin.at[i - 1, :, cols_of(n)],
            send_sem=s2send.at[n, i], recv_sem=s2recv.at[n, i],
            device_id={"tp": lax.rem(x + i, X) * 2 + core}, device_id_type=MESH,
        )

    def project(n):
        term[:, cols_of(n)] = jnp.dot(
            att[...], Wo[:, cols_of(n)], preferred_element_type=F32
        ).astype(BF)
        for xi in range(X):
            s1_copy(n, xi).start()

    def pass_on(n):
        for xi in range(X):
            s1_copy(n, xi).wait_recv()
        for i in range(1, X):
            there = lax.rem(x + i, X)
            pair[i - 1, :, cols_of(n)] = (
                term[t_rows(there * 2 + core), cols_of(n)].astype(F32)
                + sib[there, :, cols_of(n)].astype(F32)
            ).astype(BF)
            s2_copy(n, i, there).start()

    for n in range(chunks):
        project(n)
        if n:
            pass_on(n - 1)
    pass_on(chunks - 1)
    for n in range(chunks):
        total_now = term[t_rows(t), cols_of(n)].astype(F32) + sib[x, :, cols_of(n)].astype(F32)
        for i in range(1, X):
            s2_copy(n, i, x).wait_recv()
            total_now = total_now + xin[i - 1, :, cols_of(n)].astype(F32)
        out[:, cols_of(n)] = total_now.astype(BF)

    for n in range(chunks):
        for xi in range(X):
            s1_copy(n, xi).wait_send()
        for i in range(1, X):
            s2_copy(n, i, x).wait_send()
    for i in range(1, T):
        n_copy(i, t).wait_send()

    def drain(block, carry):
        for a in range(2 + parts):
            @pl.when((block <= c) & has_right)
            def _():
                z_copy(a, block, 1).wait_send()

            @pl.when((block >= c) & has_left)
            def _():
                z_copy(a, block, 0).wait_send()

            @pl.when(block != c)
            def _():
                for i in range(1, G):
                    y_copy(a, block, i, g).wait_send()

        @pl.when((block <= c) & has_right)
        def _():
            kv_copy(0, block).wait_send()
            kv_copy(1, block).wait_send()
        return carry

    lax.fori_loop(0, C, drain, 0)


def shards(G, C, T, tokens, gain, wq, wk, wv, wo, sections):
    R, D = tokens.shape
    B = R * T
    Kc, Nq = wq.shape
    Nk = wk.shape[1]
    K = Kc * C
    kv = Nk // HD
    parts = kv
    part = Nq // parts
    chunks = 4
    X = T // 2
    total = sections.shape[0]
    A = 2 + parts
    c = lax.axis_index("ctx")
    positions = c * B + jnp.arange(B, dtype=jnp.int32)
    freq = theta_base ** (-(jnp.arange(HD // 2, dtype=F32) * 2.0 / HD))
    angle = positions.astype(F32)[:, None] * freq[None, :]
    secq = lax.dynamic_slice_in_dim(sections, c * B, B)[:, None]
    vm = pl.BlockSpec(memory_space=pltpu.VMEM)
    hbm = pl.BlockSpec(memory_space=pltpu.HBM)
    dma = pltpu.SemaphoreType.DMA
    return pl.pallas_call(
        functools.partial(kernel, G, C, T, parts, chunks),
        out_shape=jax.ShapeDtypeStruct((R, D), BF),
        in_specs=[vm] * 6 + [hbm] * 4,
        out_specs=vm,
        scratch_shapes=[
            pltpu.VMEM((B, D), BF),
            pltpu.VMEM((K, Nq), BF),
            pltpu.VMEM((K, Nk), BF),
            pltpu.VMEM((K, Nk), BF),
            pltpu.VMEM(wo.shape, BF),
            pltpu.VMEM((total, Nk), BF),
            pltpu.VMEM((total, Nk), BF),
            pltpu.VMEM((part // HD, B, HD), BF),
            pltpu.VMEM((B, Nq), BF),
            pltpu.VMEM((B, D), BF),
            pltpu.VMEM((X - 1, R, D), BF),
            pltpu.VMEM((X, R, D), BF),
            pltpu.VMEM((X - 1, R, D), BF),
            dma((4,)),
            dma((A, C, 2)),
            dma((A, C)),
            dma((A, C, G)),
            dma((A, C, G)),
            dma((T,)),
            dma((T,)),
            dma((2, C)),
            dma((2, C)),
            dma((chunks, X)),
            dma((chunks, X)),
            dma((chunks, X)),
            dma((chunks, X)),
        ],
        compiler_params=pltpu.CompilerParams(
            collective_id=0, has_side_effects=True, vmem_limit_bytes=60 * 1024 * 1024
        ),
    )(tokens, gain[None, :], jnp.cos(angle), jnp.sin(angle), secq, sections[None, :],
      wq, wk, wv, wo)


def solution(mesh):
    placed = (
        P(("groups", "ctx", "tp"), None),
        P(),
        P("ctx", "tp"),
        P("ctx", "tp"),
        P("ctx", "tp"),
        P("tp", None),
        P("groups"),
    )
    return jax.shard_map(
        functools.partial(shards, mesh.shape["groups"], mesh.shape["ctx"], mesh.shape["tp"]),
        mesh=mesh,
        in_specs=placed,
        out_specs=P(("groups", "ctx", "tp"), None),
        check_vma=False,
    )
```

```python
import functools
import math

import jax
import jax.numpy as jnp
from jax import lax
from jax.experimental import pallas as pl
from jax.experimental.pallas import tpu as pltpu
from jax.sharding import PartitionSpec as P

HD = 128
MESH = pl.DeviceIdType.MESH
BF = jnp.bfloat16
F32 = jnp.float32

theta_base = 500000.0
eps_norm = 1e-05
neg_big = -1e30


def kernel(
    G, C, T, parts, chunks,
    tok, gain, cos, sin, secq, seck, wq, wk, wv, wo,
    out,
    nf, xall, acc, Wq, Wk, Wv, Wo, Kf, Vf, qbuf, att, term, pair, sib, xin,
    lsem, zsend, zrecv, ysend, yrecv, nsend, nrecv, x1send, x1recv, x2send, x2recv,
    rsend, rrecv, ksend, krecv,
    s1send, s1recv, s2send, s2recv,
):
    g = lax.axis_index("groups")
    c = lax.axis_index("ctx")
    t = lax.axis_index("tp")
    X = T // 2
    x = t // 2
    core = lax.rem(t, 2)
    R, D = tok.shape
    B = R * T
    Kc, Nq = wq.shape
    Nk = wk.shape[1]
    kv = Nk // HD
    grp = Nq // Nk
    Kh = Kc // G
    part = Nq // parts
    total = seck.shape[1]
    inv_root = 1.0 / math.sqrt(HD)
    has_right = c < C - 1
    has_left = c > 0

    own = pl.ds(pl.multiple_of(c * Kc, Kc), Kc)
    loads = [
        pltpu.make_async_copy(wk, Wk.at[own], lsem.at[0]),
        pltpu.make_async_copy(wv, Wv.at[own], lsem.at[1]),
        pltpu.make_async_copy(wq, Wq, lsem.at[2]),
        pltpu.make_async_copy(wo, Wo, lsem.at[3]),
    ]
    for load in loads:
        load.start()

    barrier = pltpu.get_barrier_semaphore()

    for i in range(1, C):
        pl.semaphore_signal(
            barrier, inc=1, device_id={"ctx": lax.rem(c + i, C)}, device_id_type=MESH
        )
    for i in range(1, G):
        pl.semaphore_signal(
            barrier, inc=1, device_id={"groups": lax.rem(g + i, G)}, device_id_type=MESH
        )
    for i in range(1, T):
        pl.semaphore_signal(
            barrier, inc=1, device_id={"tp": lax.rem(t + i, T)}, device_id_type=MESH
        )

    def t_rows(who):
        return pl.ds(pl.multiple_of(who * R, R), R)

    values = tok[...].astype(F32)
    meansq = jnp.mean(values * values, axis=-1, keepdims=True)
    nf[t_rows(t), :] = (values * lax.rsqrt(meansq + eps_norm) * gain[...]).astype(BF)
    pl.semaphore_wait(barrier, G - 1 + T - 1 + C - 1)

    def feats(who):
        return pl.ds(pl.multiple_of(who * Kc, Kc), Kc)

    def x_rows(block, who):
        return pl.ds(pl.multiple_of(block * B + who * R, R), R)

    def x1_copy(target, source):
        return pltpu.make_async_remote_copy(
            src_ref=nf.at[t_rows(t), feats(target)], dst_ref=xall.at[x_rows(source, t)],
            send_sem=x1send.at[target], recv_sem=x1recv.at[source],
            device_id={"ctx": target}, device_id_type=MESH,
        )

    def x2_copy(block, i, who):
        ref = xall.at[x_rows(block, who)]
        return pltpu.make_async_remote_copy(
            src_ref=ref, dst_ref=ref,
            send_sem=x2send.at[block, i], recv_sem=x2recv.at[block, i],
            device_id={"tp": lax.rem(t + i, T)}, device_id_type=MESH,
        )

    def farthest_first(act):
        def body(n, carry):
            far = C - 1 - n

            @pl.when(c + far < C)
            def _():
                act(c + far)

            @pl.when(c - far >= 0)
            def _():
                act(c - far)
            return carry

        lax.fori_loop(0, C - 1, body, 0)

    farthest_first(lambda target: x1_copy(target, c).start())

    def piece(a, block, half):
        rows = pl.ds(pl.multiple_of(block * Kc + half * Kh, Kh), Kh)
        if a == 0:
            return Wk.at[rows]
        return Wv.at[rows]

    def z_copy(a, block, right):
        ref = piece(a, block, g)
        return pltpu.make_async_remote_copy(
            src_ref=ref, dst_ref=ref,
            send_sem=zsend.at[a, block, right], recv_sem=zrecv.at[a, block],
            device_id={"ctx": c + 1 if right else c - 1}, device_id_type=MESH,
        )

    def y_copy(a, block, i, half):
        ref = piece(a, block, half)
        return pltpu.make_async_remote_copy(
            src_ref=ref, dst_ref=ref,
            send_sem=ysend.at[a, block, i], recv_sem=yrecv.at[a, block, i],
            device_id={"groups": lax.rem(g + i, G)}, device_id_type=MESH,
        )

    def send_own(a):
        @pl.when(has_right)
        def _():
            z_copy(a, c, 1).start()

        @pl.when(has_left)
        def _():
            z_copy(a, c, 0).start()

    def arrive(pieces, first, last):
        def body(s, carry):
            left = c - 1 - s
            right = c + 1 + s
            for a in pieces:
                @pl.when(left >= 0)
                def _():
                    z_copy(a, left, 1).wait_recv()

                    @pl.when(has_right)
                    def _():
                        z_copy(a, left, 1).start()

                    for i in range(1, G):
                        y_copy(a, left, i, g).start()

                @pl.when(right < C)
                def _():
                    z_copy(a, right, 0).wait_recv()

                    @pl.when(has_left)
                    def _():
                        z_copy(a, right, 0).start()

                    for i in range(1, G):
                        y_copy(a, right, i, g).start()
            return carry

        lax.fori_loop(first, last, body, 0)

    def y_wait(pieces):
        def body(block, carry):
            @pl.when(block != c)
            def _():
                for a in pieces:
                    for i in range(1, G):
                        y_copy(a, block, i, lax.rem(g + G - i, G)).wait_recv()
            return carry

        lax.fori_loop(0, C, body, 0)

    loads[0].wait()
    loads[1].wait()
    send_own(0)
    send_own(1)

    def share(block):
        x1_copy(block, block).wait_recv()
        for i in range(1, T):
            x2_copy(block, i, t).start()

    farthest_first(share)

    def n_copy(i, who):
        ref = nf.at[t_rows(who)]
        return pltpu.make_async_remote_copy(
            src_ref=ref, dst_ref=ref, send_sem=nsend.at[i], recv_sem=nrecv.at[i],
            device_id={"tp": lax.rem(t + i, T)}, device_id_type=MESH,
        )

    for i in range(1, T):
        n_copy(i, t).start()

    @pl.when(c == 0)
    def _():
        acc[0, :, :, :] = jnp.zeros((parts, B, part), F32)

    @pl.when(c == C - 1)
    def _():
        acc[C, :, :, :] = jnp.zeros((parts, B, part), F32)

    loads[2].wait()

    def q_copy(p, block, back):
        nbr = c + 1 - 2 * back
        slot = jnp.where((back == 1) & (nbr == block), C, block)
        return pltpu.make_async_remote_copy(
            src_ref=acc.at[block, p], dst_ref=acc.at[slot, p],
            send_sem=rsend.at[p, block], recv_sem=rrecv.at[p, slot],
            device_id={"ctx": nbr}, device_id_type=MESH,
        )

    def q_arrival(p, slot):
        return pltpu.make_async_remote_copy(
            src_ref=acc.at[slot, p], dst_ref=acc.at[slot, p],
            send_sem=rsend.at[p, 0], recv_sem=rrecv.at[p, slot],
            device_id={"ctx": c}, device_id_type=MESH,
        )

    def q_hop(p, k):
        def way(n, carry):
            back = jnp.where(2 * c >= C, 1 - n, n)
            block = jnp.where(back == 1, k, C - 1 - k)
            valid = jnp.where(back == 1, block < c, block > c)
            incoming = jnp.where(back == 1, c < C - 1, c > 0)

            @pl.when(valid)
            def _():
                if p == 0:
                    for i in range(1, T):
                        x2_copy(block, i, lax.rem(t + T - i, T)).wait_recv()
                own_sum = jnp.dot(
                    xall[pl.ds(pl.multiple_of(block * B, B), B), :],
                    Wq[:, p * part : (p + 1) * part],
                    preferred_element_type=F32,
                )

                @pl.when(incoming)
                def _():
                    q_arrival(p, block).wait_recv()
                    acc[block, p, :, :] = acc[block, p, :, :] + own_sum

                @pl.when(jnp.logical_not(incoming))
                def _():
                    acc[block, p, :, :] = own_sum

                q_copy(p, block, back).start()
            return carry

        lax.fori_loop(0, 2, way, 0)

    def first_round(k, carry):
        q_hop(0, k)
        arrive((0, 1), k, k + 1)
        return carry

    lax.fori_loop(0, C - 1, first_round, 0)
    for i in range(1, T):
        n_copy(i, lax.rem(t + T - i, T)).wait_recv()

    def rotated(head):
        a = head[:, : HD // 2]
        b = head[:, HD // 2 :]
        cs = cos[...]
        sn = sin[...]
        return jnp.concatenate([a * cs - b * sn, b * cs + a * sn], axis=-1).astype(BF)

    def kv_rows(block):
        return pl.ds(pl.multiple_of(block * B, B), B)

    def kv_copy(which, block):
        ref = (Kf, Vf)[which].at[kv_rows(block)]
        return pltpu.make_async_remote_copy(
            src_ref=ref, dst_ref=ref,
            send_sem=ksend.at[which, block], recv_sem=krecv.at[which, block],
            device_id={"ctx": c + 1}, device_id_type=MESH,
        )

    y_wait((0, 1))
    raw = jnp.dot(nf[...], Wk[...], preferred_element_type=F32)
    for j in range(kv):
        Kf[kv_rows(c), j * HD : (j + 1) * HD] = rotated(raw[:, j * HD : (j + 1) * HD])
    Vf[kv_rows(c), :] = jnp.dot(nf[...], Wv[...], preferred_element_type=F32).astype(BF)

    @pl.when(has_right)
    def _():
        kv_copy(0, c).start()
        kv_copy(1, c).start()

    def blank(block, carry):
        Kf[kv_rows(block), :] = jnp.zeros((B, Nk), BF)
        Vf[kv_rows(block), :] = jnp.zeros((B, Nk), BF)
        return carry

    lax.fori_loop(c + 1, C, blank, 0)

    def later_round(s, carry):
        for p in range(1, parts):
            q_hop(p, s)
        left = c - 1 - s

        @pl.when(left >= 0)
        def _():
            for which in range(2):
                kv_copy(which, left).wait_recv()

                @pl.when(has_right)
                def _():
                    kv_copy(which, left).start()
        return carry

    lax.fori_loop(0, C - 1, later_round, 0)

    rows_now = max(16, min(B, (256 * 1024) // total))

    def attend(j):
        @pl.when(has_left)
        def _():
            q_arrival(j, c).wait_recv()

        @pl.when(has_right)
        def _():
            q_arrival(j, C).wait_recv()

        raw = (
            jnp.dot(nf[:, feats(c)], Wq[:, j * part : (j + 1) * part], preferred_element_type=F32)
            + acc[c, j, :, :]
            + acc[C, j, :, :]
        )
        for h in range(part // HD):
            qbuf[h, :, :] = rotated(raw[:, h * HD : (h + 1) * HD])
        for h in range(part // HD):
            head = j * (part // HD) + h
            cols = slice((head // grp) * HD, (head // grp + 1) * HD)

            def tile(n, carry):
                rows = pl.ds(pl.multiple_of(n * rows_now, rows_now), rows_now)
                scores = (
                    lax.dot_general(
                        qbuf[h, rows, :], Kf[:, cols], (((1,), (1,)), ((), ())),
                        preferred_element_type=F32,
                    )
                    * inv_root
                )
                pos = c * B + n * rows_now + lax.broadcasted_iota(jnp.int32, (rows_now, total), 0)
                kpos = lax.broadcasted_iota(jnp.int32, (rows_now, total), 1)
                sq = secq[rows, :]
                sk = seck[...]
                third_q = (sq >= 3).astype(jnp.int32) + (sq >= 6).astype(jnp.int32)
                third_k = (sk >= 3).astype(jnp.int32) + (sk >= 6).astype(jnp.int32)
                prompt = sk == third_k * 3
                mask = (kpos <= pos) & (third_k == third_q) & (prompt | (sk == sq))
                scores = jnp.where(mask, scores, neg_big)
                top = jnp.max(scores, axis=-1, keepdims=True)
                weights = jnp.exp(scores - top)
                denom = jnp.sum(weights, axis=-1, keepdims=True)
                mixed = jnp.dot(weights.astype(BF), Vf[:, cols], preferred_element_type=F32)
                att[rows, head * HD : (head + 1) * HD] = (mixed / denom).astype(BF)
                return carry

            if rows_now == B:
                tile(0, 0)
            else:
                lax.fori_loop(0, B // rows_now, tile, 0)

    for j in range(parts):
        attend(j)

    loads[3].wait()
    width = D // chunks

    def cols_of(n):
        return pl.ds(n * width, width)

    def s1_copy(n, xi):
        return pltpu.make_async_remote_copy(
            src_ref=term.at[t_rows(xi * 2 + 1 - core), cols_of(n)],
            dst_ref=sib.at[xi, :, cols_of(n)],
            send_sem=s1send.at[n, xi], recv_sem=s1recv.at[n, xi],
            device_id={"tp": x * 2 + 1 - core}, device_id_type=MESH,
        )

    def s2_copy(n, i, source):
        return pltpu.make_async_remote_copy(
            src_ref=pair.at[i - 1, :, cols_of(n)],
            dst_ref=xin.at[i - 1, :, cols_of(n)],
            send_sem=s2send.at[n, i], recv_sem=s2recv.at[n, i],
            device_id={"tp": lax.rem(x + i, X) * 2 + core}, device_id_type=MESH,
        )

    def project(n):
        term[:, cols_of(n)] = jnp.dot(
            att[...], Wo[:, cols_of(n)], preferred_element_type=F32
        ).astype(BF)
        for xi in range(X):
            s1_copy(n, xi).start()

    def pass_on(n):
        for xi in range(X):
            s1_copy(n, xi).wait_recv()
        for i in range(1, X):
            there = lax.rem(x + i, X)
            pair[i - 1, :, cols_of(n)] = (
                term[t_rows(there * 2 + core), cols_of(n)].astype(F32)
                + sib[there, :, cols_of(n)].astype(F32)
            ).astype(BF)
            s2_copy(n, i, there).start()

    for n in range(chunks):
        project(n)
        if n:
            pass_on(n - 1)
    pass_on(chunks - 1)
    for n in range(chunks):
        total_now = term[t_rows(t), cols_of(n)].astype(F32) + sib[x, :, cols_of(n)].astype(F32)
        for i in range(1, X):
            s2_copy(n, i, x).wait_recv()
            total_now = total_now + xin[i - 1, :, cols_of(n)].astype(F32)
        out[:, cols_of(n)] = total_now.astype(BF)

    for n in range(chunks):
        for xi in range(X):
            s1_copy(n, xi).wait_send()
        for i in range(1, X):
            s2_copy(n, i, x).wait_send()
    for i in range(1, T):
        n_copy(i, t).wait_send()

    def drain(block, carry):
        for a in range(2):
            @pl.when((block <= c) & has_right)
            def _():
                z_copy(a, block, 1).wait_send()

            @pl.when((block >= c) & has_left)
            def _():
                z_copy(a, block, 0).wait_send()

            @pl.when(block != c)
            def _():
                for i in range(1, G):
                    y_copy(a, block, i, g).wait_send()

        @pl.when((block <= c) & has_right)
        def _():
            kv_copy(0, block).wait_send()
            kv_copy(1, block).wait_send()

        @pl.when(block != c)
        def _():
            x1_copy(block, c).wait_send()
            for i in range(1, T):
                x2_copy(block, i, t).wait_send()
            for p in range(parts):
                q_copy(p, block, (block < c).astype(jnp.int32)).wait_send()
        return carry

    lax.fori_loop(0, C, drain, 0)


def shards(G, C, T, tokens, gain, wq, wk, wv, wo, sections):
    R, D = tokens.shape
    B = R * T
    Kc, Nq = wq.shape
    Nk = wk.shape[1]
    K = Kc * C
    kv = Nk // HD
    parts = kv
    part = Nq // parts
    chunks = 4
    X = T // 2
    total = sections.shape[0]
    A = 2
    c = lax.axis_index("ctx")
    positions = c * B + jnp.arange(B, dtype=jnp.int32)
    freq = theta_base ** (-(jnp.arange(HD // 2, dtype=F32) * 2.0 / HD))
    angle = positions.astype(F32)[:, None] * freq[None, :]
    secq = lax.dynamic_slice_in_dim(sections, c * B, B)[:, None]
    vm = pl.BlockSpec(memory_space=pltpu.VMEM)
    hbm = pl.BlockSpec(memory_space=pltpu.HBM)
    dma = pltpu.SemaphoreType.DMA
    return pl.pallas_call(
        functools.partial(kernel, G, C, T, parts, chunks),
        out_shape=jax.ShapeDtypeStruct((R, D), BF),
        in_specs=[vm] * 6 + [hbm] * 4,
        out_specs=vm,
        scratch_shapes=[
            pltpu.VMEM((B, D), BF),
            pltpu.VMEM((total, Kc), BF),
            pltpu.VMEM((C + 1, parts, B, part), F32),
            pltpu.VMEM((Kc, Nq), BF),
            pltpu.VMEM((K, Nk), BF),
            pltpu.VMEM((K, Nk), BF),
            pltpu.VMEM(wo.shape, BF),
            pltpu.VMEM((total, Nk), BF),
            pltpu.VMEM((total, Nk), BF),
            pltpu.VMEM((part // HD, B, HD), BF),
            pltpu.VMEM((B, Nq), BF),
            pltpu.VMEM((B, D), BF),
            pltpu.VMEM((X - 1, R, D), BF),
            pltpu.VMEM((X, R, D), BF),
            pltpu.VMEM((X - 1, R, D), BF),
            dma((4,)),
            dma((A, C, 2)),
            dma((A, C)),
            dma((A, C, G)),
            dma((A, C, G)),
            dma((T,)),
            dma((T,)),
            dma((C,)),
            dma((C,)),
            dma((C, T)),
            dma((C, T)),
            dma((parts, C)),
            dma((parts, C + 1)),
            dma((2, C)),
            dma((2, C)),
            dma((chunks, X)),
            dma((chunks, X)),
            dma((chunks, X)),
            dma((chunks, X)),
        ],
        compiler_params=pltpu.CompilerParams(
            collective_id=0, has_side_effects=True, vmem_limit_bytes=60 * 1024 * 1024
        ),
    )(tokens, gain[None, :], jnp.cos(angle), jnp.sin(angle), secq, sections[None, :],
      wq, wk, wv, wo)


def solution(mesh):
    placed = (
        P(("groups", "ctx", "tp"), None),
        P(),
        P("ctx", "tp"),
        P("ctx", "tp"),
        P("ctx", "tp"),
        P("tp", None),
        P("groups"),
    )
    return jax.shard_map(
        functools.partial(shards, mesh.shape["groups"], mesh.shape["ctx"], mesh.shape["tp"]),
        mesh=mesh,
        in_specs=placed,
        out_specs=P(("groups", "ctx", "tp"), None),
        check_vma=False,
    )
```

```python
import functools
import math

import jax
import jax.numpy as jnp
from jax import lax
from jax.experimental import pallas as pl
from jax.experimental.pallas import tpu as pltpu
from jax.sharding import PartitionSpec as P

HD = 128
MESH = pl.DeviceIdType.MESH
BF = jnp.bfloat16
F32 = jnp.float32

theta_base = 500000.0
eps_norm = 1e-05
neg_big = -1e30


def kernel(
    G, C, T, parts, chunks,
    tok, gain, cos, sin, secq, seck, wq, wk, wv, wo,
    out,
    nf, xall, acc, Wq, Wk, Wv, Wo, Kf, Vf, qbuf, att, term, pair, sib, xin,
    lsem, zsend, zrecv, ysend, yrecv, nsend, nrecv, x1send, x1recv, x2send, x2recv,
    rsend, rrecv, ksend, krecv,
    s1send, s1recv, s2send, s2recv,
):
    g = lax.axis_index("groups")
    c = lax.axis_index("ctx")
    t = lax.axis_index("tp")
    X = T // 2
    x = t // 2
    core = lax.rem(t, 2)
    R, D = tok.shape
    B = R * T
    Kc, Nq = wq.shape
    Nk = wk.shape[1]
    kv = Nk // HD
    grp = Nq // Nk
    Kh = Kc // G
    part = Nq // parts
    total = seck.shape[1]
    inv_root = 1.0 / math.sqrt(HD)
    has_right = c < C - 1
    has_left = c > 0

    own = pl.ds(pl.multiple_of(c * Kc, Kc), Kc)
    loads = [
        pltpu.make_async_copy(wk, Wk.at[own], lsem.at[0]),
        pltpu.make_async_copy(wv, Wv.at[own], lsem.at[1]),
        pltpu.make_async_copy(wq, Wq, lsem.at[2]),
        pltpu.make_async_copy(wo, Wo, lsem.at[3]),
    ]
    for load in loads:
        load.start()

    barrier = pltpu.get_barrier_semaphore()

    for i in range(1, C):
        pl.semaphore_signal(
            barrier, inc=1, device_id={"ctx": lax.rem(c + i, C)}, device_id_type=MESH
        )
    for i in range(1, G):
        pl.semaphore_signal(
            barrier, inc=1, device_id={"groups": lax.rem(g + i, G)}, device_id_type=MESH
        )
    for i in range(1, T):
        pl.semaphore_signal(
            barrier, inc=1, device_id={"tp": lax.rem(t + i, T)}, device_id_type=MESH
        )

    def t_rows(who):
        return pl.ds(pl.multiple_of(who * R, R), R)

    values = tok[...].astype(F32)
    meansq = jnp.mean(values * values, axis=-1, keepdims=True)
    nf[t_rows(t), :] = (values * lax.rsqrt(meansq + eps_norm) * gain[...]).astype(BF)
    pl.semaphore_wait(barrier, G - 1 + T - 1 + C - 1)

    def feats(who):
        return pl.ds(pl.multiple_of(who * Kc, Kc), Kc)

    def x_rows(block, who):
        return pl.ds(pl.multiple_of(block * B + who * R, R), R)

    def x1_copy(target, source):
        return pltpu.make_async_remote_copy(
            src_ref=nf.at[t_rows(t), feats(target)], dst_ref=xall.at[x_rows(source, t)],
            send_sem=x1send.at[target], recv_sem=x1recv.at[source],
            device_id={"ctx": target}, device_id_type=MESH,
        )

    sibling = x * 2 + 1 - core

    def mate(i, k):
        return lax.rem(x + i, X) * 2 + k

    def x2_copy(block, slot, target, who):
        ref = xall.at[x_rows(block, who)]
        return pltpu.make_async_remote_copy(
            src_ref=ref, dst_ref=ref,
            send_sem=x2send.at[block, slot], recv_sem=x2recv.at[block, who],
            device_id={"tp": target}, device_id_type=MESH,
        )

    def n_copy(slot, target, who):
        ref = nf.at[t_rows(who)]
        return pltpu.make_async_remote_copy(
            src_ref=ref, dst_ref=ref, send_sem=nsend.at[slot], recv_sem=nrecv.at[who],
            device_id={"tp": target}, device_id_type=MESH,
        )

    def spread(copy):
        for i in range(1, X):
            copy(i, mate(i, core), t).start()
        copy(0, sibling, t).start()

    def spread_on(copy):
        for i in range(1, X):
            copy(0, sibling, mate(i, core)).wait_recv()
            copy(X - 1 + i, sibling, mate(i, core)).start()

    def spread_wait(copy):
        for i in range(X):
            copy(0, sibling, mate(i, 1 - core)).wait_recv()

    def spread_drain(copy):
        for i in range(2 * X - 1):
            copy(i, sibling, t).wait_send()

    def farthest_first(act):
        def body(n, carry):
            far = C - 1 - n

            @pl.when(c + far < C)
            def _():
                act(c + far)

            @pl.when(c - far >= 0)
            def _():
                act(c - far)
            return carry

        lax.fori_loop(0, C - 1, body, 0)

    farthest_first(lambda target: x1_copy(target, c).start())

    def piece(a, block, half):
        rows = pl.ds(pl.multiple_of(block * Kc + half * Kh, Kh), Kh)
        if a == 0:
            return Wk.at[rows]
        return Wv.at[rows]

    def z_copy(a, block, right):
        ref = piece(a, block, g)
        return pltpu.make_async_remote_copy(
            src_ref=ref, dst_ref=ref,
            send_sem=zsend.at[a, block, right], recv_sem=zrecv.at[a, block],
            device_id={"ctx": c + 1 if right else c - 1}, device_id_type=MESH,
        )

    def y_copy(a, block, i, half):
        ref = piece(a, block, half)
        return pltpu.make_async_remote_copy(
            src_ref=ref, dst_ref=ref,
            send_sem=ysend.at[a, block, i], recv_sem=yrecv.at[a, block, i],
            device_id={"groups": lax.rem(g + i, G)}, device_id_type=MESH,
        )

    def send_own(a):
        @pl.when(has_right)
        def _():
            z_copy(a, c, 1).start()

        @pl.when(has_left)
        def _():
            z_copy(a, c, 0).start()

    def arrive(pieces, first, last):
        def body(s, carry):
            left = c - 1 - s
            right = c + 1 + s
            for a in pieces:
                @pl.when(left >= 0)
                def _():
                    z_copy(a, left, 1).wait_recv()

                    @pl.when(has_right)
                    def _():
                        z_copy(a, left, 1).start()

                    for i in range(1, G):
                        y_copy(a, left, i, g).start()

                @pl.when(right < C)
                def _():
                    z_copy(a, right, 0).wait_recv()

                    @pl.when(has_left)
                    def _():
                        z_copy(a, right, 0).start()

                    for i in range(1, G):
                        y_copy(a, right, i, g).start()
            return carry

        lax.fori_loop(first, last, body, 0)

    def y_wait(pieces):
        def body(block, carry):
            @pl.when(block != c)
            def _():
                for a in pieces:
                    for i in range(1, G):
                        y_copy(a, block, i, lax.rem(g + G - i, G)).wait_recv()
            return carry

        lax.fori_loop(0, C, body, 0)

    loads[0].wait()
    loads[1].wait()
    send_own(0)
    send_own(1)

    def share(block):
        x1_copy(block, block).wait_recv()
        spread(functools.partial(x2_copy, block))

    farthest_first(share)
    spread(n_copy)
    farthest_first(lambda block: spread_on(functools.partial(x2_copy, block)))

    @pl.when(c == 0)
    def _():
        acc[0, :, :, :] = jnp.zeros((parts, B, part), F32)

    @pl.when(c == C - 1)
    def _():
        acc[C, :, :, :] = jnp.zeros((parts, B, part), F32)

    loads[2].wait()

    def q_copy(p, block, back):
        nbr = c + 1 - 2 * back
        slot = jnp.where((back == 1) & (nbr == block), C, block)
        return pltpu.make_async_remote_copy(
            src_ref=acc.at[block, p], dst_ref=acc.at[slot, p],
            send_sem=rsend.at[p, block], recv_sem=rrecv.at[p, slot],
            device_id={"ctx": nbr}, device_id_type=MESH,
        )

    def q_arrival(p, slot):
        return pltpu.make_async_remote_copy(
            src_ref=acc.at[slot, p], dst_ref=acc.at[slot, p],
            send_sem=rsend.at[p, 0], recv_sem=rrecv.at[p, slot],
            device_id={"ctx": c}, device_id_type=MESH,
        )

    def q_hop(p, k):
        def way(n, carry):
            back = jnp.where(2 * c >= C, 1 - n, n)
            block = jnp.where(back == 1, k, C - 1 - k)
            valid = jnp.where(back == 1, block < c, block > c)
            incoming = jnp.where(back == 1, c < C - 1, c > 0)

            @pl.when(valid)
            def _():
                if p == 0:
                    spread_wait(functools.partial(x2_copy, block))
                own_sum = jnp.dot(
                    xall[pl.ds(pl.multiple_of(block * B, B), B), :],
                    Wq[:, p * part : (p + 1) * part],
                    preferred_element_type=F32,
                )

                @pl.when(incoming)
                def _():
                    q_arrival(p, block).wait_recv()
                    acc[block, p, :, :] = acc[block, p, :, :] + own_sum

                @pl.when(jnp.logical_not(incoming))
                def _():
                    acc[block, p, :, :] = own_sum

                q_copy(p, block, back).start()
            return carry

        lax.fori_loop(0, 2, way, 0)

    is_end = jnp.logical_or(c == 0, c == C - 1)
    early = max(C - 2, 1)

    def hops(p, first, last):
        def body(k, carry):
            q_hop(p, k)
            return carry

        lax.fori_loop(first, last, body, 0)

    def phase(n, carry):
        @pl.when(is_end == (n == 0))
        def _():
            hops(0, 0, C - 1)

            @pl.when(is_end)
            def _():
                for p in range(1, parts):
                    hops(p, 0, early)

        @pl.when(n == 0)
        def _():
            arrive((0, 1), 0, C - 1)
        return carry

    lax.fori_loop(0, 2, phase, 0)
    spread_on(n_copy)
    spread_wait(n_copy)

    def rotated(head):
        a = head[:, : HD // 2]
        b = head[:, HD // 2 :]
        cs = cos[...]
        sn = sin[...]
        return jnp.concatenate([a * cs - b * sn, b * cs + a * sn], axis=-1).astype(BF)

    def kv_rows(block):
        return pl.ds(pl.multiple_of(block * B, B), B)

    def kv_copy(which, block):
        ref = (Kf, Vf)[which].at[kv_rows(block)]
        return pltpu.make_async_remote_copy(
            src_ref=ref, dst_ref=ref,
            send_sem=ksend.at[which, block], recv_sem=krecv.at[which, block],
            device_id={"ctx": c + 1}, device_id_type=MESH,
        )

    y_wait((0, 1))
    raw = jnp.dot(nf[...], Wk[...], preferred_element_type=F32)
    for j in range(kv):
        Kf[kv_rows(c), j * HD : (j + 1) * HD] = rotated(raw[:, j * HD : (j + 1) * HD])
    Vf[kv_rows(c), :] = jnp.dot(nf[...], Wv[...], preferred_element_type=F32).astype(BF)

    @pl.when(has_right)
    def _():
        kv_copy(0, c).start()
        kv_copy(1, c).start()

    def blank(block, carry):
        Kf[kv_rows(block), :] = jnp.zeros((B, Nk), BF)
        Vf[kv_rows(block), :] = jnp.zeros((B, Nk), BF)
        return carry

    lax.fori_loop(c + 1, C, blank, 0)

    def later_round(s, carry):
        for p in range(1, parts):
            @pl.when(jnp.logical_not(is_end) | (s >= early))
            def _():
                q_hop(p, s)
        left = c - 1 - s

        @pl.when(left >= 0)
        def _():
            for which in range(2):
                kv_copy(which, left).wait_recv()

                @pl.when(has_right)
                def _():
                    kv_copy(which, left).start()
        return carry

    lax.fori_loop(0, C - 1, later_round, 0)

    rows_now = max(16, min(B, (256 * 1024) // total))

    def attend(j):
        @pl.when(has_left)
        def _():
            q_arrival(j, c).wait_recv()

        @pl.when(has_right)
        def _():
            q_arrival(j, C).wait_recv()

        raw = (
            jnp.dot(nf[:, feats(c)], Wq[:, j * part : (j + 1) * part], preferred_element_type=F32)
            + acc[c, j, :, :]
            + acc[C, j, :, :]
        )
        for h in range(part // HD):
            qbuf[h, :, :] = rotated(raw[:, h * HD : (h + 1) * HD])
        for h in range(part // HD):
            head = j * (part // HD) + h
            cols = slice((head // grp) * HD, (head // grp + 1) * HD)

            def tile(n, carry):
                rows = pl.ds(pl.multiple_of(n * rows_now, rows_now), rows_now)
                scores = (
                    lax.dot_general(
                        qbuf[h, rows, :], Kf[:, cols], (((1,), (1,)), ((), ())),
                        preferred_element_type=F32,
                    )
                    * inv_root
                )
                pos = c * B + n * rows_now + lax.broadcasted_iota(jnp.int32, (rows_now, total), 0)
                kpos = lax.broadcasted_iota(jnp.int32, (rows_now, total), 1)
                sq = secq[rows, :]
                sk = seck[...]
                third_q = (sq >= 3).astype(jnp.int32) + (sq >= 6).astype(jnp.int32)
                third_k = (sk >= 3).astype(jnp.int32) + (sk >= 6).astype(jnp.int32)
                prompt = sk == third_k * 3
                mask = (kpos <= pos) & (third_k == third_q) & (prompt | (sk == sq))
                scores = jnp.where(mask, scores, neg_big)
                top = jnp.max(scores, axis=-1, keepdims=True)
                weights = jnp.exp(scores - top)
                denom = jnp.sum(weights, axis=-1, keepdims=True)
                mixed = jnp.dot(weights.astype(BF), Vf[:, cols], preferred_element_type=F32)
                att[rows, head * HD : (head + 1) * HD] = (mixed / denom).astype(BF)
                return carry

            if rows_now == B:
                tile(0, 0)
            else:
                lax.fori_loop(0, B // rows_now, tile, 0)

    for j in range(parts):
        attend(j)

    loads[3].wait()
    width = D // chunks

    def cols_of(n):
        return pl.ds(n * width, width)

    def s1_copy(n, xi):
        return pltpu.make_async_remote_copy(
            src_ref=term.at[t_rows(xi * 2 + 1 - core), cols_of(n)],
            dst_ref=sib.at[xi, :, cols_of(n)],
            send_sem=s1send.at[n, xi], recv_sem=s1recv.at[n, xi],
            device_id={"tp": x * 2 + 1 - core}, device_id_type=MESH,
        )

    def s2_copy(n, i, source):
        return pltpu.make_async_remote_copy(
            src_ref=pair.at[i - 1, :, cols_of(n)],
            dst_ref=xin.at[i - 1, :, cols_of(n)],
            send_sem=s2send.at[n, i], recv_sem=s2recv.at[n, i],
            device_id={"tp": lax.rem(x + i, X) * 2 + core}, device_id_type=MESH,
        )

    def project(n):
        term[:, cols_of(n)] = jnp.dot(
            att[...], Wo[:, cols_of(n)], preferred_element_type=F32
        ).astype(BF)
        for xi in range(X):
            s1_copy(n, xi).start()

    def pass_on(n):
        for xi in range(X):
            s1_copy(n, xi).wait_recv()
        for i in range(1, X):
            there = lax.rem(x + i, X)
            pair[i - 1, :, cols_of(n)] = (
                term[t_rows(there * 2 + core), cols_of(n)].astype(F32)
                + sib[there, :, cols_of(n)].astype(F32)
            ).astype(BF)
            s2_copy(n, i, there).start()

    for n in range(chunks):
        project(n)
        if n:
            pass_on(n - 1)
    pass_on(chunks - 1)
    for n in range(chunks):
        total_now = term[t_rows(t), cols_of(n)].astype(F32) + sib[x, :, cols_of(n)].astype(F32)
        for i in range(1, X):
            s2_copy(n, i, x).wait_recv()
            total_now = total_now + xin[i - 1, :, cols_of(n)].astype(F32)
        out[:, cols_of(n)] = total_now.astype(BF)

    for n in range(chunks):
        for xi in range(X):
            s1_copy(n, xi).wait_send()
        for i in range(1, X):
            s2_copy(n, i, x).wait_send()
    spread_drain(n_copy)

    def drain(block, carry):
        for a in range(2):
            @pl.when((block <= c) & has_right)
            def _():
                z_copy(a, block, 1).wait_send()

            @pl.when((block >= c) & has_left)
            def _():
                z_copy(a, block, 0).wait_send()

            @pl.when(block != c)
            def _():
                for i in range(1, G):
                    y_copy(a, block, i, g).wait_send()

        @pl.when((block <= c) & has_right)
        def _():
            kv_copy(0, block).wait_send()
            kv_copy(1, block).wait_send()

        @pl.when(block != c)
        def _():
            x1_copy(block, c).wait_send()
            spread_drain(functools.partial(x2_copy, block))
            for p in range(parts):
                q_copy(p, block, (block < c).astype(jnp.int32)).wait_send()
        return carry

    lax.fori_loop(0, C, drain, 0)


def shards(G, C, T, tokens, gain, wq, wk, wv, wo, sections):
    R, D = tokens.shape
    B = R * T
    Kc, Nq = wq.shape
    Nk = wk.shape[1]
    K = Kc * C
    kv = Nk // HD
    parts = kv
    part = Nq // parts
    chunks = 4
    X = T // 2
    total = sections.shape[0]
    A = 2
    c = lax.axis_index("ctx")
    positions = c * B + jnp.arange(B, dtype=jnp.int32)
    freq = theta_base ** (-(jnp.arange(HD // 2, dtype=F32) * 2.0 / HD))
    angle = positions.astype(F32)[:, None] * freq[None, :]
    secq = lax.dynamic_slice_in_dim(sections, c * B, B)[:, None]
    vm = pl.BlockSpec(memory_space=pltpu.VMEM)
    hbm = pl.BlockSpec(memory_space=pltpu.HBM)
    dma = pltpu.SemaphoreType.DMA
    return pl.pallas_call(
        functools.partial(kernel, G, C, T, parts, chunks),
        out_shape=jax.ShapeDtypeStruct((R, D), BF),
        in_specs=[vm] * 6 + [hbm] * 4,
        out_specs=vm,
        scratch_shapes=[
            pltpu.VMEM((B, D), BF),
            pltpu.VMEM((total, Kc), BF),
            pltpu.VMEM((C + 1, parts, B, part), F32),
            pltpu.VMEM((Kc, Nq), BF),
            pltpu.VMEM((K, Nk), BF),
            pltpu.VMEM((K, Nk), BF),
            pltpu.VMEM(wo.shape, BF),
            pltpu.VMEM((total, Nk), BF),
            pltpu.VMEM((total, Nk), BF),
            pltpu.VMEM((part // HD, B, HD), BF),
            pltpu.VMEM((B, Nq), BF),
            pltpu.VMEM((B, D), BF),
            pltpu.VMEM((X - 1, R, D), BF),
            pltpu.VMEM((X, R, D), BF),
            pltpu.VMEM((X - 1, R, D), BF),
            dma((4,)),
            dma((A, C, 2)),
            dma((A, C)),
            dma((A, C, G)),
            dma((A, C, G)),
            dma((T,)),
            dma((T,)),
            dma((C,)),
            dma((C,)),
            dma((C, T)),
            dma((C, T)),
            dma((parts, C)),
            dma((parts, C + 1)),
            dma((2, C)),
            dma((2, C)),
            dma((chunks, X)),
            dma((chunks, X)),
            dma((chunks, X)),
            dma((chunks, X)),
        ],
        compiler_params=pltpu.CompilerParams(
            collective_id=0, has_side_effects=True, vmem_limit_bytes=60 * 1024 * 1024
        ),
    )(tokens, gain[None, :], jnp.cos(angle), jnp.sin(angle), secq, sections[None, :],
      wq, wk, wv, wo)


def solution(mesh):
    placed = (
        P(("groups", "ctx", "tp"), None),
        P(),
        P("ctx", "tp"),
        P("ctx", "tp"),
        P("ctx", "tp"),
        P("tp", None),
        P("groups"),
    )
    return jax.shard_map(
        functools.partial(shards, mesh.shape["groups"], mesh.shape["ctx"], mesh.shape["tp"]),
        mesh=mesh,
        in_specs=placed,
        out_specs=P(("groups", "ctx", "tp"), None),
        check_vma=False,
    )
```
